32 devices in a mesh: pole: 2 (over y), prow: 4 (over z), pcol: 4 (over x, core).
Axes of the slice: x: 2, y: 2, z: 4, core: 2. Of those that a mesh axis runs over, the one named last changes fastest.
Arguments:
- known_inverse: bfloat16 [4096, 2048], P(('pole', 'prow'), 'pcol'), parts along dimension 0, may hold values from -6 to 6
- upper_panel: bfloat16 [32, 4, 128, 128], P(('pole', 'prow'), 'pcol'), parts along dimension 0, may hold values from -0.125 to 0.125
- upper_slots: int32 [16, 4], P('prow', 'pcol'), may hold values from -1 to 3, as said below
- upper_pivots: float32 [1024, 128], P(('pole', 'prow', 'pcol')), parts along dimension 0, may hold values from -6 to 6
- lower_panel: bfloat16 [32, 4, 128, 128], P(('pole', 'prow'), 'pcol'), parts along dimension 0, may hold values from -0.125 to 0.125
- lower_slots: int32 [16, 4], P('prow', 'pcol'), may hold values from -1 to 4, as said below
- lower_pivots: float32 [1024, 128], P(('pole', 'prow', 'pcol')), parts along dimension 0, may hold values from -6 to 6
Outputs:
- upper_rows: bfloat16 [1024, 2048], P(('pole', 'prow'), 'pcol'), parts along dimension 0
- upper_diagonal: float32 [1024, 128], P(('pole', 'prow', 'pcol')), parts along dimension 0
- lower_rows: bfloat16 [1024, 2048], P(('pole', 'prow'), 'pcol'), parts along dimension 0
- lower_diagonal: float32 [1024, 128], P(('pole', 'prow', 'pcol')), parts along dimension 0
The draws below stay inside these ranges and needn't reach their ends.
There are 2 independent parts, one for each index of `pole`. The reference program is written for one: setup_inputs(seed, part) draws one part's arguments, and reference() takes and returns one part's arrays. A program takes and returns all parts, laid end to end along the dimension named above; an argument that names none is the same for every part. Nothing has to cross between parts.
Inputs may be any that keep to these rules, and one draw needn't show every extreme that they name: `upper_slots`: rows r*4 to r*4 + 3 of a column k form supernode k's list on process row r: distinct values, live entries first, -1 marking an empty slot; value v names ancestor r*4+v. `lower_slots`: rows r*4 to r*4 + 3 of a column k form supernode k's list on process row r: distinct values, live entries first, -1 marking an empty slot; value v below 4 names ancestor r*4+v, value 4 names upper-level supernode r. The first entry of row floor(k)*4 is always 4, and 4 appears nowhere else.
All inputs are finite; a program needn't handle non-finite values.
Results may differ from the reference program's by a relative error of at most 0.006.
Values may be sent and summed in bfloat16 or wider, within the bound.
No kernel may reach another device: no remote copies, remote signals or barrier semaphores. Data moves between devices by JAX's collectives and lax.ppermute only.
A program may use at most 64 MiB of HBM per device.

```python
import jax
import jax.numpy as jnp
from jax import lax

B = 128
AR = 4
CH = 1
NA = 16
N2 = 4
N1 = 4


def slot_lists(key, column_total, with_parent):
    score_key, count_key = jax.random.split(key)
    scores = jax.random.randint(score_key, (N2, column_total, AR), 0, 1 << 20) * AR + jnp.arange(AR, dtype=jnp.int32)
    ordering = jnp.argsort(scores, axis=-1, stable=True).astype(jnp.int32)
    live_count = jax.random.randint(count_key, (N2, column_total), 0, AR + 1)
    live_count = live_count.at[0, 0].set(AR).at[0, 1].set(1)
    position = jnp.arange(AR, dtype=jnp.int32)
    if with_parent == 1:
        owner_row = jnp.arange(column_total, dtype=jnp.int32) // CH
        is_parent = jnp.arange(N2, dtype=jnp.int32)[:, None] == owner_row[None, :]
        shifted = jnp.concatenate([jnp.full((N2, column_total, 1), AR, jnp.int32), ordering[:, :, :AR - 1]], axis=2)
        ordering = jnp.where(is_parent[:, :, None], shifted, ordering)
        live_count = jnp.where(is_parent, jnp.maximum(live_count, 1), live_count)
    chosen = jnp.where(position < live_count[:, :, None], ordering, -1)
    return jnp.transpose(chosen, (0, 2, 1)).reshape(N2 * AR, column_total).astype(jnp.int32)


def draw_upper_slots(key, part):
    key = jax.random.fold_in(key, 11)
    return slot_lists(key, N2, 0)


def draw_lower_slots(key, part):
    key = jax.random.fold_in(key, 12)
    return slot_lists(key, N1, 1)


def block_levels(own_key, shape, pieces, low, largest):
    def one(dim, shards_of):
        draws = jax.random.uniform(jax.random.fold_in(jax.random.fold_in(own_key, 6), dim), (shards_of,), jnp.float32, low / len(pieces), largest / len(pieces))
        return jnp.repeat(jnp.exp(draws), shape[dim] // shards_of).reshape((-1,) + (1,) * (len(shape) - dim - 1))

    level = one(*pieces[0])
    for cut in pieces[1:]:
        level = level * one(*cut)
    return level


def bell_draw(rng, shape, width, limit, cuts=(), kind=jnp.bfloat16):
    loudness = block_levels(rng, shape, cuts, -0.22, 0.18) if cuts else 1.0
    result = jax.random.normal(rng, shape, jnp.float32) * width * loudness
    return jnp.minimum(jnp.maximum(result, -limit), limit).astype(kind)


def setup_inputs(seed: int = 0, part: int = 0) -> dict:
    seeds = jax.random.split(jax.random.key(seed), 8)
    part_splits = jax.random.split(jax.random.fold_in(seeds[7], part), 8)
    known_inverse = bell_draw(part_splits[0], (NA * B, NA * B), 1.0, 6.0, ((0, 4), (1, 4)))
    upper_panel = bell_draw(part_splits[1], (N2 * AR, N2, B, B), (NA * B) ** -0.5, 0.125, ((0, 4), (1, 4)))
    upper_slots = draw_upper_slots(jax.random.fold_in(seeds[7], 71), part)
    upper_pivots = bell_draw(part_splits[3], (N2 * B, B), 1.0, 6.0, ((0, 16),), jnp.float32)
    lower_panel = bell_draw(part_splits[4], (N2 * AR, N1, B, B), (NA * B) ** -0.5, 0.125, ((0, 4), (1, 4)))
    lower_slots = draw_lower_slots(jax.random.fold_in(seeds[7], 71), part)
    lower_pivots = bell_draw(part_splits[6], (N1 * B, B), 1.0, 6.0, ((0, 16),), jnp.float32)
    return dict(known_inverse=known_inverse, upper_panel=upper_panel, upper_slots=upper_slots, upper_pivots=upper_pivots, lower_panel=lower_panel, lower_slots=lower_slots, lower_pivots=lower_pivots)


precise = lax.Precision.HIGHEST


def spread_panel(blocks, slot_index, extent):
    columns = blocks.shape[1]
    block_side = blocks.shape[2]
    grouped = blocks.reshape(N2, AR, columns, block_side, block_side).astype(jnp.float32)
    chosen = slot_index.reshape(N2, AR, columns)
    selector = (chosen[:, :, :, None] == jnp.arange(extent, dtype=jnp.int32)).astype(jnp.float32)
    expanded = jnp.einsum("rska,rskij->raikj", selector, grouped)
    return expanded.reshape(N2 * extent * block_side, columns * block_side).astype(jnp.bfloat16)


def reference(known_inverse, upper_panel, upper_slots, upper_pivots, lower_panel, lower_slots, lower_pivots):
    numbers = (((0,), (0,)), ((), ()))
    upper_full = spread_panel(upper_panel, upper_slots, AR)
    upper_sum = lax.dot_general(upper_full, known_inverse, numbers, preferred_element_type=jnp.float32)
    upper_rows = (-upper_sum).astype(jnp.bfloat16)
    upper_cols = upper_full.astype(jnp.float32).reshape(NA * B, N2, B)
    upper_terms = jnp.einsum("kin,nkj->kij", upper_sum.reshape(N2, B, NA * B), upper_cols, precision=precise)
    upper_diagonal = upper_pivots + upper_terms.reshape(N2 * B, B)
    extended = jnp.concatenate([known_inverse.reshape(N2, AR * B, NA * B), upper_rows.reshape(N2, B, NA * B)], axis=1)
    extended = extended.reshape(N2 * (AR + 1) * B, NA * B)
    lower_full = spread_panel(lower_panel, lower_slots, AR + 1)
    lower_sum = lax.dot_general(lower_full, extended, numbers, preferred_element_type=jnp.float32)
    lower_rows = (-lower_sum).astype(jnp.bfloat16)
    lower_ancestors = spread_panel(lower_panel, lower_slots, AR).astype(jnp.float32).reshape(NA * B, N1, B)
    first_term = jnp.einsum("kin,nkj->kij", lower_sum.reshape(N1, B, NA * B), lower_ancestors, precision=precise)
    supernode = jnp.arange(N1, dtype=jnp.int32)
    parent = supernode // CH
    parent_panel = lower_panel[parent * AR, supernode].astype(jnp.float32)
    parent_rows = upper_rows.reshape(N2, B, NA * B)[parent].astype(jnp.float32)
    coupling = jnp.einsum("kin,nkj->kij", parent_rows, lower_ancestors, precision=precise)
    parent_diag = upper_diagonal.reshape(N2, B, B)[parent]
    side_block = jnp.swapaxes(coupling, 1, 2) + jnp.einsum("kai,kaj->kij", parent_panel, parent_diag, precision=precise)
    second_term = jnp.einsum("kia,kaj->kij", side_block, parent_panel, precision=precise)
    lower_diagonal = lower_pivots + (first_term + second_term).reshape(N1 * B, B)
    return upper_rows, upper_diagonal, lower_rows, lower_diagonal
```

```python
import functools

import jax
import jax.numpy as jnp
from jax import lax
from jax.experimental import pallas as pl
from jax.experimental.pallas import tpu as pltpu
from jax.sharding import PartitionSpec as P

AR = 4
BF = jnp.bfloat16
F32 = jnp.float32
VMEM = pl.BlockSpec(memory_space=pltpu.VMEM)
SMEM = pl.BlockSpec(memory_space=pltpu.SMEM)


def tdot(a, b):
    return lax.dot_general(a, b, (((0,), (0,)), ((), ())), preferred_element_type=F32)


def ndot(a, b):
    return lax.dot_general(a, b, (((1,), (0,)), ((), ())), preferred_element_type=F32)


def split(x):
    hi = x.astype(BF)
    return hi, (x - hi.astype(F32)).astype(BF)


def spread(dense, row_start, panel, column, slots, slot_start):
    side = panel.shape[2]
    for s in range(AR):
        v = slots[slot_start + s, column]

        @pl.when((v >= 0) & (v < AR))
        def _():
            rows = pl.ds(pl.multiple_of(row_start + v * side, side), side)
            dense[rows, :] = panel[s, column]


def partial_kernel(prow, pcol, columns, slot_start, with_parent, *refs):
    panels, refs = refs[:pcol], refs[pcol:]
    slots, refs = refs[:pcol], refs[pcol:]
    known, refs = refs[0], refs[1:]
    outs, refs = refs[:prow], refs[prow:]
    dense = refs[-1]
    r = lax.axis_index("prow")
    c = lax.axis_index("pcol")
    side = panels[0].shape[2]
    extent = AR * side
    dense[...] = jnp.zeros_like(dense)
    for j in range(pcol):
        for i in range(columns):
            k = (c ^ j) * columns + i
            spread(dense, k * extent, panels[j], i, slots[j], slot_start)
            if with_parent:

                @pl.when(k == r)
                def _():
                    refs[0][...] = panels[j][0, i]

    for t in range(prow):
        rows = pl.ds(pl.multiple_of((r ^ t) * extent, extent), extent)
        outs[t][...] = tdot(dense[rows, :], known[...]).astype(outs[t].dtype)


def finish_kernel(prow, pcol, columns, *refs):
    upper_parts, refs = refs[:prow], refs[prow:]
    lower_parts, refs = refs[:prow], refs[prow:]
    upper_turned, refs = refs[:columns], refs[columns:]
    lower_turned, refs = refs[:columns], refs[columns:]
    slots_turned, refs = refs[:columns], refs[columns:]
    parent_ref, pivots, refs = refs[0], refs[1], refs[2:]
    upper_rows, lower_rows, refs = refs[0], refs[1], refs[2:]
    pieces, refs = refs[:pcol], refs[pcol:]
    dense, parts = refs
    r = lax.axis_index("prow")
    c = lax.axis_index("pcol")
    side = parent_ref.shape[0]
    extent = AR * side
    share = pivots.shape[0]
    dense[...] = jnp.zeros_like(dense)
    for p in range(columns):
        q = (r - p) % columns if columns > 1 else 0
        spread(dense.at[0], q * extent, upper_turned[p], 0, slots_turned[p], 0)
        spread(dense.at[1], q * extent, lower_turned[p], 0, slots_turned[p], AR)
    parent = parent_ref[...]
    upper_sum = upper_parts[0][...]
    for t in range(1, prow):
        upper_sum += upper_parts[t][...].astype(F32)
    hi, lo = split(upper_sum)
    rows = -hi
    upper_rows[...] = rows
    upper_part = ndot(hi, dense[0]) + ndot(lo, dense[0])
    parts[0] = upper_part
    parts[1] = upper_part
    own = pl.ds(pl.multiple_of(c * share, share), share)
    parts[1, own, :] += pivots[...]
    lower_sum = lower_parts[0][...] + tdot(parent, rows)
    for t in range(1, prow):
        lower_sum += lower_parts[t][...].astype(F32)
    hi, lo = split(lower_sum)
    lower_rows[...] = -hi
    lower_part = ndot(hi, dense[1]) + ndot(lo, dense[1])
    coupling_hi, coupling_lo = split(ndot(rows, dense[1]))
    lower_part += tdot(coupling_hi, parent) + tdot(coupling_lo, parent)
    hi, lo = split(parts[1])
    hi, lo = split(ndot(hi, parent) + ndot(lo, parent))
    parts[1] = lower_part + tdot(parent, hi) + tdot(parent, lo)
    for s in range(pcol):
        theirs = pl.ds(pl.multiple_of((c ^ s) * share, share), share)
        pieces[s][0] = parts[0, theirs, :].astype(pieces[s].dtype)
        pieces[s][1] = parts[1, theirs, :].astype(pieces[s].dtype)


def sum_kernel(pcol, *refs):
    pieces, refs = refs[:pcol], refs[pcol:]
    upper_pivots, lower_pivots, upper_diagonal, lower_diagonal = refs
    total = pieces[0][...]
    for s in range(1, pcol):
        total += pieces[s][...].astype(F32)
    upper_diagonal[...] = upper_pivots[...] + total[0]
    lower_diagonal[...] = lower_pivots[...] + total[1]


def call(kernel, outs, specs, scratch=()):
    return pl.pallas_call(
        kernel,
        out_shape=outs,
        in_specs=specs,
        out_specs=tuple(VMEM for _ in outs),
        scratch_shapes=scratch,
        compiler_params=pltpu.CompilerParams(vmem_limit_bytes=48 << 20),
    )


def per_device(
    known_inverse, upper_panel, upper_slots, upper_pivots, lower_panel, lower_slots, lower_pivots
):
    prow = lax.axis_size("prow")
    pcol = lax.axis_size("pcol")
    columns = upper_panel.shape[1]
    side = upper_panel.shape[2]
    width = known_inverse.shape[1]
    extent = AR * side
    share = upper_pivots.shape[0]
    shape = jax.ShapeDtypeStruct

    def across(x, j):
        return lax.ppermute(x, "pcol", [(c, c ^ j) for c in range(pcol)])

    def along(x, t):
        return lax.ppermute(x, "prow", [(r, r ^ t) for r in range(prow)])

    def gather(x):
        held = {0: x}
        for j in range(2, pcol, 2):
            held[j] = across(x, j)
        for j in range(1, pcol, 2):
            held[j] = across(held[j - 1], 1)
        return [held[j] for j in range(pcol)]

    def turned(x):
        moved = []
        for p in range(columns):
            pairs = []
            for a in range(prow):
                for b in range(pcol):
                    pairs.append((a * pcol + b, (b * columns + (a + p) % columns) * pcol + a // columns))
            piece = x
            if columns > 1:
                first = (lax.axis_index("prow") + p) % columns
                piece = lax.dynamic_slice_in_dim(x, first, 1, 1)
            moved.append(lax.ppermute(piece, ("prow", "pcol"), pairs))
        return moved

    slots = jnp.concatenate([upper_slots, lower_slots], axis=0)
    upper_all = gather(upper_panel)
    lower_all = gather(lower_panel)
    slots_all = gather(slots)
    upper_turned = turned(upper_panel)
    lower_turned = turned(lower_panel)
    slots_turned = turned(slots)

    def partial(panels, slot_start, with_parent):
        outs = [shape((side, width), F32)] + [shape((side, width), BF)] * (prow - 1)
        if with_parent:
            outs.append(shape((side, side), BF))
        return call(
            functools.partial(partial_kernel, prow, pcol, columns, slot_start, with_parent),
            tuple(outs),
            [VMEM] * pcol + [SMEM] * pcol + [VMEM],
            [pltpu.VMEM((prow * extent, side), BF)],
        )(*panels, *slots_all, known_inverse)

    upper_parts = partial(upper_all, 0, False)
    lower_parts = partial(lower_all, AR, True)
    parent = lower_parts[-1]
    upper_sent = [upper_parts[0]] + [along(upper_parts[t], t) for t in range(1, prow)]
    lower_sent = [lower_parts[0]] + [along(lower_parts[t], t) for t in range(1, prow)]
    outs = [shape((side, width), BF)] * 2 + [shape((2, share, side), F32)]
    outs += [shape((2, share, side), BF)] * (pcol - 1)
    finished = call(
        functools.partial(finish_kernel, prow, pcol, columns),
        tuple(outs),
        [VMEM] * (2 * prow + 2 * columns) + [SMEM] * columns + [VMEM] * 2,
        [pltpu.VMEM((2, width, side), BF), pltpu.VMEM((2, side, side), F32)],
    )(*upper_sent, *lower_sent, *upper_turned, *lower_turned, *slots_turned, parent, upper_pivots)
    upper_rows, lower_rows = finished[:2]
    pieces = [finished[2]] + [across(finished[2 + s], s) for s in range(1, pcol)]
    upper_diagonal, lower_diagonal = call(
        functools.partial(sum_kernel, pcol),
        (shape((share, side), F32), shape((share, side), F32)),
        [VMEM] * (pcol + 2),
    )(*pieces, upper_pivots, lower_pivots)
    return upper_rows, upper_diagonal, lower_rows, lower_diagonal


def solution(mesh):
    placed = (
        P(("pole", "prow"), "pcol"),
        P(("pole", "prow"), "pcol", None, None),
        P("prow", "pcol"),
        P(("pole", "prow", "pcol"), None),
        P(("pole", "prow"), "pcol", None, None),
        P("prow", "pcol"),
        P(("pole", "prow", "pcol"), None),
    )
    return jax.shard_map(
        per_device,
        mesh=mesh,
        in_specs=placed,
        out_specs=(
            P(("pole", "prow"), "pcol"),
            P(("pole", "prow", "pcol"), None),
            P(("pole", "prow"), "pcol"),
            P(("pole", "prow", "pcol"), None),
        ),
        check_vma=False,
    )
```

```python
import functools

import jax
import jax.numpy as jnp
from jax import lax
from jax.experimental import pallas as pl
from jax.experimental.pallas import tpu as pltpu
from jax.sharding import PartitionSpec as P

AR = 4
BF = jnp.bfloat16
F32 = jnp.float32
VMEM = pl.BlockSpec(memory_space=pltpu.VMEM)
HBM = pl.BlockSpec(memory_space=pltpu.HBM)
SMEM = pl.BlockSpec(memory_space=pltpu.SMEM)


def tdot(a, b):
    return lax.dot_general(a, b, (((0,), (0,)), ((), ())), preferred_element_type=F32)


def ndot(a, b):
    return lax.dot_general(a, b, (((1,), (0,)), ((), ())), preferred_element_type=F32)


def split(x):
    hi = x.astype(BF)
    return hi, (x - hi.astype(F32)).astype(BF)


def place(dense, panel, column, slots):
    for s in range(AR):
        v = slots[column, s]

        @pl.when((v >= 0) & (v < AR))
        def _():
            dense[v] = panel[s, column]


def pack_kernel(
    columns, upper_far, lower_far, upper_slots, lower_slots, packed, turned, upper, lower, arrived
):
    copies = [
        pltpu.make_async_copy(upper_far, upper, arrived.at[0]),
        pltpu.make_async_copy(lower_far, lower, arrived.at[1]),
    ]
    for copy in copies:
        copy.start()
    packed[...] = jnp.zeros_like(packed)
    for copy in copies:
        copy.wait()
    for i in range(columns):
        place(packed.at[i, :AR], upper, i, upper_slots)
        place(packed.at[i, AR : 2 * AR], lower, i, lower_slots)
        packed[i, 2 * AR] = lower[0, i]
        turned[i] = packed[i, : 2 * AR]


def holder(k, columns):
    return (k // columns) % 2


def rounds(prow, columns):
    sends = [(t, e) for t in range(prow) for e in range(2) if (t, e) != (0, 0)]
    lists = {}
    for t, e in sends:
        lists.setdefault(((t // columns) % 2, e), []).append((t, e))
    out = []
    for e in range(2):
        even, odd = lists[0, e][::-1], lists[1, 1 - e][::-1]
        for n in range(max(len(even), len(odd))):
            out.append((even[n] if n < len(even) else None, odd[n] if n < len(odd) else None))
    return out


def partial_kernel(plan, columns, halves, *refs):
    packed, refs = refs[:halves], refs[halves:]
    own_known, other_known, refs = refs[0], refs[1], refs[2:]
    own, refs = refs[0], refs[1:]
    outs, refs = refs[: len(plan)], refs[len(plan) :]
    parent, dense, known = refs
    r = lax.axis_index("prow")
    c = lax.axis_index("pcol")
    side = parent.shape[0]
    extent = AR * side
    holds = c % 2 == holder(r, columns)

    def slot(k):
        return k // (2 * columns) * columns + k % columns

    known[0] = own_known[...]
    known[1] = other_known[...]
    for j in range(halves):
        for i in range(columns):
            k = (c ^ (2 * j)) * columns + i
            for level in range(2):
                blocks = packed[j][i, level * AR : (level + 1) * AR]
                dense[slot(k), :, level * side : (level + 1) * side] = blocks.reshape(extent, side)

            @pl.when(k == r)
            def _():
                parent[...] = packed[j][i, 2 * AR]

    for n, (even, odd) in enumerate(plan):

        def put(t, e):
            outs[n][...] = tdot(dense[slot(r ^ t)], known[e]).astype(BF)

        if even is None or odd is None:

            @pl.when(holds if odd is None else jnp.logical_not(holds))
            def _():
                put(*(even or odd))

        else:
            put(jnp.where(holds, even[0], odd[0]), jnp.where(holds, even[1], odd[1]))

    @pl.when(holds)
    def _():
        own[...] = tdot(dense[slot(r)], own_known[...])

    @pl.when(jnp.logical_not(holds))
    def _():
        own[...] = jnp.zeros_like(own)
        parent[...] = jnp.zeros_like(parent)


def finish_kernel(count, pcol, columns, *refs):
    sums, refs = refs[:count], refs[count:]
    turned, refs = refs[:columns], refs[columns:]
    parent_ref, parent_other, pivots, refs = refs[0], refs[1], refs[2], refs[3:]
    upper_rows, lower_rows, refs = refs[0], refs[1], refs[2:]
    pieces, refs = refs[:pcol], refs[pcol:]
    dense, parts = refs
    r = lax.axis_index("prow")
    c = lax.axis_index("pcol")
    side = parent_ref.shape[0]
    extent = AR * side
    share = pivots.shape[0]
    for p in range(columns):
        q = (r - p) % columns if columns > 1 else 0
        for level in range(2):
            rows = pl.ds(pl.multiple_of(q * extent, extent), extent)
            blocks = turned[p][0, level * AR : (level + 1) * AR]
            dense[level, rows, :] = blocks.reshape(extent, side)
    parent = parent_ref[...] + parent_other[...]
    upper_sum = sums[0][:side]
    lower_sum = sums[0][side:]
    for t in range(1, count):
        upper_sum += sums[t][:side].astype(F32)
        lower_sum += sums[t][side:].astype(F32)
    hi, lo = split(upper_sum)
    rows = -hi
    upper_rows[...] = rows
    upper_part = ndot(hi, dense[0]) + ndot(lo, dense[0])
    parts[0] = upper_part
    parts[1] = upper_part
    own = pl.ds(pl.multiple_of(c * share, share), share)
    parts[1, own, :] += pivots[...]
    lower_sum += tdot(parent, rows)
    hi, lo = split(lower_sum)
    lower_rows[...] = -hi
    lower_part = ndot(hi, dense[1]) + ndot(lo, dense[1])
    coupling_hi, coupling_lo = split(ndot(rows, dense[1]))
    lower_part += tdot(coupling_hi, parent) + tdot(coupling_lo, parent)
    hi, lo = split(parts[1])
    hi, lo = split(ndot(hi, parent) + ndot(lo, parent))
    parts[1] = lower_part + tdot(parent, hi) + tdot(parent, lo)
    for s in range(pcol):
        theirs = pl.ds(pl.multiple_of((c ^ s) * share, share), share)
        pieces[s][0] = parts[0, theirs, :].astype(pieces[s].dtype)
        pieces[s][1] = parts[1, theirs, :].astype(pieces[s].dtype)


def sum_kernel(pcol, *refs):
    pieces, refs = refs[:pcol], refs[pcol:]
    upper_pivots, lower_pivots, upper_diagonal, lower_diagonal = refs
    total = pieces[0][...]
    for s in range(1, pcol):
        total += pieces[s][...].astype(F32)
    upper_diagonal[...] = upper_pivots[...] + total[0]
    lower_diagonal[...] = lower_pivots[...] + total[1]


def call(kernel, outs, specs, scratch=(), room=32):
    return pl.pallas_call(
        kernel,
        out_shape=outs,
        in_specs=specs,
        out_specs=tuple(VMEM for _ in outs),
        scratch_shapes=scratch,
        cost_estimate=pl.CostEstimate(flops=0, bytes_accessed=0, transcendentals=0),
        compiler_params=pltpu.CompilerParams(vmem_limit_bytes=room << 20),
    )


def per_device(
    known_inverse, upper_panel, upper_slots, upper_pivots, lower_panel, lower_slots, lower_pivots
):
    prow = lax.axis_size("prow")
    pcol = lax.axis_size("pcol")
    columns = upper_panel.shape[1]
    side = upper_panel.shape[2]
    width = known_inverse.shape[1]
    extent = AR * side
    share = upper_pivots.shape[0]
    shape = jax.ShapeDtypeStruct

    def across(x, j):
        return lax.ppermute(x, "pcol", [(c, c ^ j) for c in range(pcol)])

    def flat(r, c):
        return r * pcol + c

    def send(x, even, odd):
        pairs = []
        for r in range(prow):
            for c in range(pcol):
                step = even if c % 2 == holder(r, columns) else odd
                if step is not None:
                    pairs.append((flat(r, c), flat(r ^ step[0], c ^ step[1])))
        return lax.ppermute(x, ("prow", "pcol"), pairs)

    def turned(x):
        moved = []
        for p in range(columns):
            pairs = []
            for a in range(prow):
                for b in range(pcol):
                    pairs.append((a * pcol + b, (b * columns + (a + p) % columns) * pcol + a // columns))
            piece = x
            if columns > 1:
                first = (lax.axis_index("prow") + p) % columns
                piece = lax.dynamic_slice_in_dim(x, first, 1, 0)
            moved.append(lax.ppermute(piece, ("prow", "pcol"), pairs))
        return moved

    packed, packed_own = call(
        functools.partial(pack_kernel, columns),
        (
            shape((columns, 2 * AR + 1, side, side), BF),
            shape((columns, 2 * AR, side, side), BF),
        ),
        [HBM] * 2 + [SMEM] * 2,
        [pltpu.VMEM(upper_panel.shape, BF)] * 2 + [pltpu.SemaphoreType.DMA((2,))],
        60,
    )(upper_panel, lower_panel, upper_slots.T, lower_slots.T)
    packed_all = [packed] + [across(packed, j) for j in range(2, pcol, 2)]
    other_known = across(known_inverse, 1)
    packed_turned = turned(packed_own)
    plan = rounds(prow, columns)
    outs = [shape((2 * side, width), F32)] + [shape((2 * side, width), BF)] * len(plan)
    *sums, parent = call(
        functools.partial(partial_kernel, plan, columns, pcol // 2),
        tuple(outs) + (shape((side, side), BF),),
        [VMEM] * (pcol // 2 + 2),
        [
            pltpu.VMEM((prow // 2, extent, 2 * side), BF),
            pltpu.VMEM((2,) + known_inverse.shape, BF),
        ],
    )(*packed_all, known_inverse, other_known)
    sums = [sums[0]] + [send(x, *steps) for x, steps in zip(sums[1:], plan)]
    parent_other = across(parent, 1)
    outs = [shape((side, width), BF)] * 2 + [shape((2, share, side), F32)]
    outs += [shape((2, share, side), BF)] * (pcol - 1)
    finished = call(
        functools.partial(finish_kernel, len(sums), pcol, columns),
        tuple(outs),
        [VMEM] * (len(sums) + columns + 3),
        [pltpu.VMEM((2, width, side), BF), pltpu.VMEM((2, side, side), F32)],
    )(*sums, *packed_turned, parent, parent_other, upper_pivots)
    upper_rows, lower_rows = finished[:2]
    pieces = [finished[2]] + [across(finished[2 + s], s) for s in range(1, pcol)]
    upper_diagonal, lower_diagonal = call(
        functools.partial(sum_kernel, pcol),
        (shape((share, side), F32), shape((share, side), F32)),
        [VMEM] * (pcol + 2),
    )(*pieces, upper_pivots, lower_pivots)
    return upper_rows, upper_diagonal, lower_rows, lower_diagonal


def solution(mesh):
    placed = (
        P(("pole", "prow"), "pcol"),
        P(("pole", "prow"), "pcol", None, None),
        P("prow", "pcol"),
        P(("pole", "prow", "pcol"), None),
        P(("pole", "prow"), "pcol", None, None),
        P("prow", "pcol"),
        P(("pole", "prow", "pcol"), None),
    )
    return jax.shard_map(
        per_device,
        mesh=mesh,
        in_specs=placed,
        out_specs=(
            P(("pole", "prow"), "pcol"),
            P(("pole", "prow", "pcol"), None),
            P(("pole", "prow"), "pcol"),
            P(("pole", "prow", "pcol"), None),
        ),
        check_vma=False,
    )
```

```python
import functools

import jax
import jax.numpy as jnp
from jax import lax
from jax.experimental import pallas as pl
from jax.experimental.pallas import tpu as pltpu
from jax.sharding import PartitionSpec as P

AR = 4
TURN_FLOPS = 4 << 30
BF = jnp.bfloat16
F32 = jnp.float32
VMEM = pl.BlockSpec(memory_space=pltpu.VMEM)
HBM = pl.BlockSpec(memory_space=pltpu.HBM)
SMEM = pl.BlockSpec(memory_space=pltpu.SMEM)


def tdot(a, b):
    return lax.dot_general(a, b, (((0,), (0,)), ((), ())), preferred_element_type=F32)


def ndot(a, b):
    return lax.dot_general(a, b, (((1,), (0,)), ((), ())), preferred_element_type=F32)


def split(x):
    hi = x.astype(BF)
    return hi, (x - hi.astype(F32)).astype(BF)


def place(dense, panel, column, slots):
    for s in range(AR):
        v = slots[column, s]

        @pl.when((v >= 0) & (v < AR))
        def _():
            dense[v] = panel[s, column]


def pack_kernel(
    columns, upper_far, lower_far, upper_slots, lower_slots, packed, turned, upper, lower, arrived
):
    copies = [
        pltpu.make_async_copy(upper_far, upper, arrived.at[0]),
        pltpu.make_async_copy(lower_far, lower, arrived.at[1]),
    ]
    for copy in copies:
        copy.start()
    packed[...] = jnp.zeros_like(packed)
    for copy in copies:
        copy.wait()
    for i in range(columns):
        place(packed.at[i, :AR], upper, i, upper_slots)
        place(packed.at[i, AR : 2 * AR], lower, i, lower_slots)
        packed[i, 2 * AR] = lower[0, i]
        turned[i] = packed[i, : 2 * AR]


def holder(k, columns):
    return (k // columns) % 2


def rounds(prow, columns):
    sends = [(t, e) for t in range(prow) for e in range(2) if (t, e) != (0, 0)]
    lists = {}
    for t, e in sends:
        lists.setdefault(((t // columns) % 2, e), []).append((t, e))
    out = []
    for e in range(2):
        even, odd = lists[0, e][::-1], lists[1, 1 - e][::-1]
        for n in range(max(len(even), len(odd))):
            out.append((even[n] if n < len(even) else None, odd[n] if n < len(odd) else None))
    return out


def partial_kernel(plan, columns, halves, *refs):
    packed, refs = refs[:halves], refs[halves:]
    own_known, other_known, refs = refs[0], refs[1], refs[2:]
    own, refs = refs[0], refs[1:]
    outs, refs = refs[: len(plan)], refs[len(plan) :]
    parent, dense, known = refs
    r = lax.axis_index("prow")
    c = lax.axis_index("pcol")
    side = parent.shape[0]
    extent = AR * side
    holds = c % 2 == holder(r, columns)

    def slot(k):
        return k // (2 * columns) * columns + k % columns

    known[0] = own_known[...]
    known[1] = other_known[...]
    for j in range(halves):
        for i in range(columns):
            k = (c ^ (2 * j)) * columns + i
            for level in range(2):
                blocks = packed[j][i, level * AR : (level + 1) * AR]
                dense[slot(k), :, level * side : (level + 1) * side] = blocks.reshape(extent, side)

            @pl.when(k == r)
            def _():
                parent[...] = packed[j][i, 2 * AR]

    for n, (even, odd) in enumerate(plan):

        def put(t, e):
            outs[n][...] = tdot(dense[slot(r ^ t)], known[e]).astype(BF)

        if even is None or odd is None:

            @pl.when(holds if odd is None else jnp.logical_not(holds))
            def _():
                put(*(even or odd))

        else:
            put(jnp.where(holds, even[0], odd[0]), jnp.where(holds, even[1], odd[1]))

    @pl.when(holds)
    def _():
        own[...] = tdot(dense[slot(r)], own_known[...])

    @pl.when(jnp.logical_not(holds))
    def _():
        own[...] = jnp.zeros_like(own)
        parent[...] = jnp.zeros_like(parent)


def halving_kernel(columns, halves, *refs):
    packed, refs = refs[:halves], refs[halves:]
    own_known, other_known, first, second, third, fourth, own, parent, dense = refs
    r = lax.axis_index("prow")
    c = lax.axis_index("pcol")
    side = parent.shape[0]
    extent = AR * side
    holds = c % 2 == holder(r, columns)

    def slot(k):
        return k // (2 * columns) * columns + k % columns

    for j in range(halves):
        for i in range(columns):
            k = (c ^ (2 * j)) * columns + i
            for level in range(2):
                blocks = packed[j][i, level * AR : (level + 1) * AR]
                dense[slot(k), :, level * side : (level + 1) * side] = blocks.reshape(extent, side)

            @pl.when(k == r)
            def _():
                parent[...] = packed[j][i, 2 * AR]

    @pl.when(holds)
    def _():
        panel = dense[slot(r)]
        first[...] = tdot(panel, other_known[...]).astype(BF)
        own[...] = tdot(panel, own_known[...])
        second[:side, :side] = parent[...]
        panel = dense[slot(r ^ 2)]
        third[...] = tdot(panel, own_known[...])
        fourth[...] = tdot(panel, other_known[...])

    @pl.when(jnp.logical_not(holds))
    def _():
        panel = dense[slot(r ^ 3)]
        first[...] = tdot(panel, own_known[...]).astype(BF)
        second[...] = tdot(panel, other_known[...]).astype(BF)
        panel = dense[slot(r ^ 1)]
        third[...] = tdot(panel, other_known[...])
        fourth[...] = tdot(panel, own_known[...])


def add_kernel(columns, kept, arrived, total):
    holds = lax.axis_index("pcol") % 2 == holder(lax.axis_index("prow"), columns)

    @pl.when(holds)
    def _():
        total[...] = (kept[...] + arrived[...].astype(F32)).astype(BF)

    @pl.when(jnp.logical_not(holds))
    def _():
        total[...] = kept[...].astype(BF)


def turn_kernel(columns, *refs):
    turned, dense = refs[:-1], refs[-1]
    r = lax.axis_index("prow")
    side = dense.shape[2]
    extent = AR * side
    for p in range(columns):
        q = (r - p) % columns if columns > 1 else 0
        for level in range(2):
            rows = pl.ds(pl.multiple_of(q * extent, extent), extent)
            blocks = turned[p][0, level * AR : (level + 1) * AR]
            dense[level, rows, :] = blocks.reshape(extent, side)


def finish_kernel(halving, count, pcol, columns, *refs):
    sums, refs = refs[:count], refs[count:]
    dense, parent_ref, parent_other, pivots, refs = refs[0], refs[1], refs[2], refs[3], refs[4:]
    upper_rows, lower_rows, refs = refs[0], refs[1], refs[2:]
    pieces, refs = refs[:pcol], refs[pcol:]
    parts = refs[0]
    r = lax.axis_index("prow")
    c = lax.axis_index("pcol")
    side = parent_ref.shape[0]
    share = pivots.shape[0]
    if halving:
        holds = c % 2 == holder(r, columns)
        parent = jnp.where(holds, parent_ref[...], parent_other[:side, :side])
        total = jnp.where(holds, sums[0][...], sums[1][...].astype(F32))
        total += sums[2][...].astype(F32) + sums[3][...].astype(F32)
    else:
        parent = parent_ref[...] + parent_other[...]
        total = sums[0][...]
        for t in range(1, count):
            total += sums[t][...].astype(F32)
    upper_sum, lower_sum = total[:side], total[side:]
    hi, lo = split(upper_sum)
    rows = -hi
    upper_rows[...] = rows
    upper_part = ndot(hi, dense[0]) + ndot(lo, dense[0])
    parts[0] = upper_part
    parts[1] = upper_part
    own = pl.ds(pl.multiple_of(c * share, share), share)
    parts[1, own, :] += pivots[...]
    lower_sum += tdot(parent, rows)
    hi, lo = split(lower_sum)
    lower_rows[...] = -hi
    lower_part = ndot(hi, dense[1]) + ndot(lo, dense[1])
    coupling_hi, coupling_lo = split(ndot(rows, dense[1]))
    lower_part += tdot(coupling_hi, parent) + tdot(coupling_lo, parent)
    hi, lo = split(parts[1])
    hi, lo = split(ndot(hi, parent) + ndot(lo, parent))
    parts[1] = lower_part + tdot(parent, hi) + tdot(parent, lo)
    for s in range(pcol):
        theirs = pl.ds(pl.multiple_of((c ^ s) * share, share), share)
        pieces[s][0] = parts[0, theirs, :].astype(pieces[s].dtype)
        pieces[s][1] = parts[1, theirs, :].astype(pieces[s].dtype)


def sum_kernel(pcol, *refs):
    pieces, refs = refs[:pcol], refs[pcol:]
    upper_pivots, lower_pivots, upper_diagonal, lower_diagonal = refs
    total = pieces[0][...]
    for s in range(1, pcol):
        total += pieces[s][...].astype(F32)
    upper_diagonal[...] = upper_pivots[...] + total[0]
    lower_diagonal[...] = lower_pivots[...] + total[1]


def call(kernel, outs, specs, scratch=(), room=32, flops=0):
    return pl.pallas_call(
        kernel,
        out_shape=outs,
        in_specs=specs,
        out_specs=tuple(VMEM for _ in outs),
        scratch_shapes=scratch,
        cost_estimate=pl.CostEstimate(flops=flops, bytes_accessed=0, transcendentals=0),
        compiler_params=pltpu.CompilerParams(vmem_limit_bytes=room << 20),
    )


def per_device(
    known_inverse, upper_panel, upper_slots, upper_pivots, lower_panel, lower_slots, lower_pivots
):
    prow = lax.axis_size("prow")
    pcol = lax.axis_size("pcol")
    columns = upper_panel.shape[1]
    side = upper_panel.shape[2]
    width = known_inverse.shape[1]
    extent = AR * side
    share = upper_pivots.shape[0]
    shape = jax.ShapeDtypeStruct

    def across(x, j):
        return lax.ppermute(x, "pcol", [(c, c ^ j) for c in range(pcol)])

    def flat(r, c):
        return r * pcol + c

    def send(x, even, odd):
        pairs = []
        for r in range(prow):
            for c in range(pcol):
                step = even if c % 2 == holder(r, columns) else odd
                if step is not None:
                    pairs.append((flat(r, c), flat(r ^ step[0], c ^ step[1])))
        return lax.ppermute(x, ("prow", "pcol"), pairs)

    def trade(x, held_step, held_other, step, other):
        pairs = []
        for r in range(prow):
            for c in range(pcol):
                if c % 2 == holder(r, columns):
                    pairs.append((flat(r, c), flat(r ^ held_step, c ^ held_other)))
                else:
                    pairs.append((flat(r, c), flat(r ^ step, c ^ other)))
        return lax.ppermute(x, ("prow", "pcol"), pairs)

    def add(kept, arrived):
        out = (shape(arrived.shape, BF),)
        return call(functools.partial(add_kernel, columns), out, [VMEM] * 2)(kept, arrived)[0]

    def turn(moved):
        return call(
            functools.partial(turn_kernel, columns),
            (shape((2, width, side), BF),),
            [VMEM] * columns,
            flops=TURN_FLOPS,
        )(*moved)[0]

    def turned(x):
        moved = []
        for p in range(columns):
            pairs = []
            for a in range(prow):
                for b in range(pcol):
                    pairs.append((a * pcol + b, (b * columns + (a + p) % columns) * pcol + a // columns))
            piece = x
            if columns > 1:
                first = (lax.axis_index("prow") + p) % columns
                piece = lax.dynamic_slice_in_dim(x, first, 1, 0)
            moved.append(lax.ppermute(piece, ("prow", "pcol"), pairs))
        return moved

    packed, packed_own = call(
        functools.partial(pack_kernel, columns),
        (
            shape((columns, 2 * AR + 1, side, side), BF),
            shape((columns, 2 * AR, side, side), BF),
        ),
        [HBM] * 2 + [SMEM] * 2,
        [pltpu.VMEM(upper_panel.shape, BF)] * 2 + [pltpu.SemaphoreType.DMA((2,))],
        60,
    )(upper_panel, lower_panel, upper_slots.T, lower_slots.T)
    packed_all = [packed] + [across(packed, j) for j in range(2, pcol, 2)]
    other_known = across(known_inverse, 1)
    packed_turned = turned(packed_own)
    part = (2 * side, width)
    halving = prow == 4 and columns == 1
    if halving:
        first, second, third, fourth, own, parent = call(
            functools.partial(halving_kernel, columns, pcol // 2),
            (shape(part, BF), shape(part, BF), shape(part, F32), shape(part, F32))
            + (shape(part, F32), shape((side, side), BF)),
            [VMEM] * (pcol // 2 + 2),
            [pltpu.VMEM((prow // 2, extent, 2 * side), BF)],
        )(*packed_all, known_inverse, other_known)
        first = trade(first, 0, 1, 1, 0)
        parent_other = trade(second, 0, 1, 1, 0)
        dense_turned = turn(packed_turned)
        first, dense_turned = lax.optimization_barrier((first, dense_turned))
        third = trade(add(third, first), 2, 0, 1, 1)
        fourth = trade(add(fourth, parent_other), 2, 1, 1, 0)
        sums = [own, first, third, fourth]
    else:
        plan = rounds(prow, columns)
        outs = [shape((2 * side, width), F32)] + [shape((2 * side, width), BF)] * len(plan)
        *sums, parent = call(
            functools.partial(partial_kernel, plan, columns, pcol // 2),
            tuple(outs) + (shape((side, side), BF),),
            [VMEM] * (pcol // 2 + 2),
            [
                pltpu.VMEM((prow // 2, extent, 2 * side), BF),
                pltpu.VMEM((2,) + known_inverse.shape, BF),
            ],
        )(*packed_all, known_inverse, other_known)
        sums = [sums[0]] + [send(x, *steps) for x, steps in zip(sums[1:], plan)]
        parent_other = across(parent, 1)
        dense_turned = turn(packed_turned)
    outs = [shape((side, width), BF)] * 2 + [shape((2, share, side), F32)]
    outs += [shape((2, share, side), BF)] * (pcol - 1)
    finished = call(
        functools.partial(finish_kernel, halving, len(sums), pcol, columns),
        tuple(outs),
        [VMEM] * (len(sums) + 4),
        [pltpu.VMEM((2, side, side), F32)],
    )(*sums, dense_turned, parent, parent_other, upper_pivots)
    upper_rows, lower_rows = finished[:2]
    pieces = [finished[2]] + [across(finished[2 + s], s) for s in range(1, pcol)]
    upper_diagonal, lower_diagonal = call(
        functools.partial(sum_kernel, pcol),
        (shape((share, side), F32), shape((share, side), F32)),
        [VMEM] * (pcol + 2),
    )(*pieces, upper_pivots, lower_pivots)
    return upper_rows, upper_diagonal, lower_rows, lower_diagonal


def solution(mesh):
    placed = (
        P(("pole", "prow"), "pcol"),
        P(("pole", "prow"), "pcol", None, None),
        P("prow", "pcol"),
        P(("pole", "prow", "pcol"), None),
        P(("pole", "prow"), "pcol", None, None),
        P("prow", "pcol"),
        P(("pole", "prow", "pcol"), None),
    )
    return jax.shard_map(
        per_device,
        mesh=mesh,
        in_specs=placed,
        out_specs=(
            P(("pole", "prow"), "pcol"),
            P(("pole", "prow", "pcol"), None),
            P(("pole", "prow"), "pcol"),
            P(("pole", "prow", "pcol"), None),
        ),
        check_vma=False,
    )
```

```python
import functools

import jax
import jax.numpy as jnp
from jax import lax
from jax.experimental import pallas as pl
from jax.experimental.pallas import tpu as pltpu
from jax.sharding import PartitionSpec as P

AR = 4
TURN_FLOPS = 1 << 28
NEAR_FLOPS = 1 << 30
BF = jnp.bfloat16
F32 = jnp.float32
VMEM = pl.BlockSpec(memory_space=pltpu.VMEM)
HBM = pl.BlockSpec(memory_space=pltpu.HBM)
SMEM = pl.BlockSpec(memory_space=pltpu.SMEM)


def tdot(a, b):
    return lax.dot_general(a, b, (((0,), (0,)), ((), ())), preferred_element_type=F32)


def ndot(a, b):
    return lax.dot_general(a, b, (((1,), (0,)), ((), ())), preferred_element_type=F32)


def split(x):
    hi = x.astype(BF)
    return hi, (x - hi.astype(F32)).astype(BF)


def lay(dense, panel, slots_ref, level):
    side = panel.shape[-1]
    slots = slots_ref[...].astype(F32)
    for v in range(AR):
        total = None
        for s in range(AR):
            index = level * AR + s
            chosen = (slots[index : index + 1] == v).astype(BF)
            term = panel[s * side : (s + 1) * side, :] * chosen
            total = term if total is None else total + term
        dense[v * side : (v + 1) * side, :] = total


def copy_kernel(known, near):
    near[...] = known[...]


def holder(k, columns):
    return (k // columns) % 2


def rounds(prow, columns):
    sends = [(t, e) for t in range(prow) for e in range(2) if (t, e) != (0, 0)]
    lists = {}
    for t, e in sends:
        lists.setdefault(((t // columns) % 2, e), []).append((t, e))
    out = []
    for e in range(2):
        even, odd = lists[0, e][::-1], lists[1, 1 - e][::-1]
        for n in range(max(len(even), len(odd))):
            out.append((even[n] if n < len(even) else None, odd[n] if n < len(odd) else None))
    return out


def partial_kernel(plan, columns, halves, *refs):
    panels = refs[:halves], refs[halves : 2 * halves]
    slots, refs = refs[2 * halves : 3 * halves], refs[3 * halves :]
    own_known, other_known, refs = refs[0], refs[1], refs[2:]
    own, refs = refs[0], refs[1:]
    outs, refs = refs[: len(plan)], refs[len(plan) :]
    parent, dense, known = refs
    r = lax.axis_index("prow")
    c = lax.axis_index("pcol")
    side = parent.shape[0]
    extent = AR * side
    holds = c % 2 == holder(r, columns)

    def slot(k):
        return k // (2 * columns) * columns + k % columns

    known[0] = own_known[...]
    known[1] = other_known[...]
    for j in range(halves):
        for i in range(columns):
            k = (c ^ (2 * j)) * columns + i
            for level in range(2):
                columns_of = pl.ds(level * side, side)
                lay(dense.at[slot(k), :, columns_of], panels[level][j].at[i], slots[j].at[i], level)

            @pl.when(k == r)
            def _():
                parent[...] = panels[1][j][i, :side]

    for n, (even, odd) in enumerate(plan):

        def put(t, e):
            outs[n][...] = tdot(dense[slot(r ^ t)], known[e]).astype(BF)

        if even is None or odd is None:

            @pl.when(holds if odd is None else jnp.logical_not(holds))
            def _():
                put(*(even or odd))

        else:
            put(jnp.where(holds, even[0], odd[0]), jnp.where(holds, even[1], odd[1]))

    @pl.when(holds)
    def _():
        own[...] = tdot(dense[slot(r)], own_known[...])

    @pl.when(jnp.logical_not(holds))
    def _():
        own[...] = jnp.zeros_like(own)
        parent[...] = jnp.zeros_like(parent)


def halving_kernel(columns, halves, *refs):
    panels = refs[:halves], refs[halves : 2 * halves]
    slots, refs = refs[2 * halves : 3 * halves], refs[3 * halves :]
    own_known, other_known, first, second, third, fourth, own, parent, dense = refs
    r = lax.axis_index("prow")
    c = lax.axis_index("pcol")
    side = parent.shape[0]
    extent = AR * side
    holds = c % 2 == holder(r, columns)

    def slot(k):
        return k // (2 * columns) * columns + k % columns

    for j in range(halves):
        for i in range(columns):
            k = (c ^ (2 * j)) * columns + i
            for level in range(2):
                columns_of = pl.ds(level * side, side)
                lay(dense.at[slot(k), :, columns_of], panels[level][j].at[i], slots[j].at[i], level)

            @pl.when(k == r)
            def _():
                parent[...] = panels[1][j][i, :side]

    @pl.when(holds)
    def _():
        panel = dense[slot(r)]
        first[...] = tdot(panel, other_known[...]).astype(BF)
        own[...] = tdot(panel, own_known[...])
        second[:side, :side] = parent[...]
        panel = dense[slot(r ^ 2)]
        third[...] = tdot(panel, own_known[...])
        fourth[...] = tdot(panel, other_known[...])

    @pl.when(jnp.logical_not(holds))
    def _():
        panel = dense[slot(r ^ 3)]
        first[...] = tdot(panel, own_known[...]).astype(BF)
        second[...] = tdot(panel, other_known[...]).astype(BF)
        panel = dense[slot(r ^ 1)]
        third[...] = tdot(panel, other_known[...])
        fourth[...] = tdot(panel, own_known[...])


def add_kernel(columns, kept, arrived, total):
    holds = lax.axis_index("pcol") % 2 == holder(lax.axis_index("prow"), columns)

    @pl.when(holds)
    def _():
        total[...] = (kept[...] + arrived[...].astype(F32)).astype(BF)

    @pl.when(jnp.logical_not(holds))
    def _():
        total[...] = kept[...].astype(BF)


def turn_kernel(columns, *refs):
    turned, dense = refs[:-1], refs[-1]
    r = lax.axis_index("prow")
    side = dense.shape[2]
    extent = AR * side
    for p in range(columns):
        q = (r - p) % columns if columns > 1 else 0
        for level in range(2):
            rows = pl.ds(pl.multiple_of(q * extent, extent), extent)
            panel = turned[p].at[0, pl.ds(level * extent, extent), :]
            slots = turned[p].at[0, pl.ds(2 * extent, 4 * AR), :]
            lay(dense.at[level, rows, :], panel, slots, level)


def finish_kernel(halving, count, pcol, columns, *refs):
    sums, refs = refs[:count], refs[count:]
    dense, parent_ref, parent_other, pivots, refs = refs[0], refs[1], refs[2], refs[3], refs[4:]
    upper_rows, lower_rows, refs = refs[0], refs[1], refs[2:]
    pieces, refs = refs[:pcol], refs[pcol:]
    parts = refs[0]
    r = lax.axis_index("prow")
    c = lax.axis_index("pcol")
    side = parent_ref.shape[0]
    share = pivots.shape[0]
    if halving:
        holds = c % 2 == holder(r, columns)
        parent = jnp.where(holds, parent_ref[...], parent_other[:side, :side])
        total = jnp.where(holds, sums[0][...], sums[1][...].astype(F32))
        total += sums[2][...].astype(F32) + sums[3][...].astype(F32)
    else:
        parent = parent_ref[...] + parent_other[...]
        total = sums[0][...]
        for t in range(1, count):
            total += sums[t][...].astype(F32)
    upper_sum, lower_sum = total[:side], total[side:]
    hi, lo = split(upper_sum)
    rows = -hi
    upper_rows[...] = rows
    upper_part = ndot(hi, dense[0]) + ndot(lo, dense[0])
    parts[0] = upper_part
    parts[1] = upper_part
    own = pl.ds(pl.multiple_of(c * share, share), share)
    parts[1, own, :] += pivots[...]
    lower_sum += tdot(parent, rows)
    hi, lo = split(lower_sum)
    lower_rows[...] = -hi
    lower_part = ndot(hi, dense[1]) + ndot(lo, dense[1])
    coupling_hi, coupling_lo = split(ndot(rows, dense[1]))
    lower_part += tdot(coupling_hi, parent) + tdot(coupling_lo, parent)
    hi, lo = split(parts[1])
    hi, lo = split(ndot(hi, parent) + ndot(lo, parent))
    parts[1] = lower_part + tdot(parent, hi) + tdot(parent, lo)
    for s in range(pcol):
        theirs = pl.ds(pl.multiple_of((c ^ s) * share, share), share)
        pieces[s][0] = parts[0, theirs, :].astype(pieces[s].dtype)
        pieces[s][1] = parts[1, theirs, :].astype(pieces[s].dtype)


def sum_kernel(pcol, *refs):
    pieces, refs = refs[:pcol], refs[pcol:]
    upper_pivots, lower_pivots, upper_diagonal, lower_diagonal = refs
    total = pieces[0][...]
    for s in range(1, pcol):
        total += pieces[s][...].astype(F32)
    upper_diagonal[...] = upper_pivots[...] + total[0]
    lower_diagonal[...] = lower_pivots[...] + total[1]


def call(kernel, outs, specs, scratch=(), room=32, flops=0):
    return pl.pallas_call(
        kernel,
        out_shape=outs,
        in_specs=specs,
        out_specs=tuple(VMEM for _ in outs),
        scratch_shapes=scratch,
        cost_estimate=pl.CostEstimate(flops=flops, bytes_accessed=0, transcendentals=0),
        compiler_params=pltpu.CompilerParams(vmem_limit_bytes=room << 20),
    )


def per_device(
    known_inverse, upper_panel, upper_slots, upper_pivots, lower_panel, lower_slots, lower_pivots
):
    prow = lax.axis_size("prow")
    pcol = lax.axis_size("pcol")
    columns = upper_panel.shape[1]
    side = upper_panel.shape[2]
    width = known_inverse.shape[1]
    extent = AR * side
    share = upper_pivots.shape[0]
    shape = jax.ShapeDtypeStruct

    def across(x, j):
        return lax.ppermute(x, "pcol", [(c, c ^ j) for c in range(pcol)])

    def flat(r, c):
        return r * pcol + c

    def send(x, even, odd):
        pairs = []
        for r in range(prow):
            for c in range(pcol):
                step = even if c % 2 == holder(r, columns) else odd
                if step is not None:
                    pairs.append((flat(r, c), flat(r ^ step[0], c ^ step[1])))
        return lax.ppermute(x, ("prow", "pcol"), pairs)

    def swing(x):
        pairs = []
        for a in range(prow):
            for b in range(pcol):
                c = a ^ 2 if a // 2 == b // 2 else b // 2 * 2 + a % 2
                pairs.append((flat(a, b), flat(b, c)))
        return lax.ppermute(x, ("prow", "pcol"), pairs)

    def trade(x, held_step, held_other, step, other):
        pairs = []
        for r in range(prow):
            for c in range(pcol):
                if c % 2 == holder(r, columns):
                    pairs.append((flat(r, c), flat(r ^ held_step, c ^ held_other)))
                else:
                    pairs.append((flat(r, c), flat(r ^ step, c ^ other)))
        return lax.ppermute(x, ("prow", "pcol"), pairs)

    def add(kept, arrived):
        out = (shape(arrived.shape, BF),)
        return call(functools.partial(add_kernel, columns), out, [VMEM] * 2)(kept, arrived)[0]

    def turn(moved):
        return call(
            functools.partial(turn_kernel, columns),
            (shape((2, width, side), BF),),
            [VMEM] * columns,
            flops=TURN_FLOPS,
        )(*moved)[0]

    def turned(x):
        moved = []
        for p in range(columns):
            pairs = []
            for a in range(prow):
                for b in range(pcol):
                    pairs.append((a * pcol + b, (b * columns + (a + p) % columns) * pcol + a // columns))
            piece = x
            if columns > 1:
                first = (lax.axis_index("prow") + p) % columns
                piece = lax.dynamic_slice_in_dim(x, first, 1, 0)
            moved.append(lax.ppermute(piece, ("prow", "pcol"), pairs))
        return moved

    slots = jnp.concatenate([upper_slots, lower_slots, lower_slots, lower_slots], axis=0).T
    packed = [
        jnp.swapaxes(upper_panel, 0, 1).reshape(columns, extent, side),
        jnp.swapaxes(lower_panel, 0, 1).reshape(columns, extent, side),
        jnp.broadcast_to(slots[:, :, None].astype(BF), (columns, 4 * AR, side)),
    ]
    packed_all = []
    for x in packed:
        packed_all += [x] + [across(x, j) for j in range(2, pcol, 2)]
    other_known = across(known_inverse, 1)
    near = call(copy_kernel, (shape(known_inverse.shape, BF),), [VMEM], flops=NEAR_FLOPS)(known_inverse)[0]
    halving = prow == 4 and columns == 1
    whole = jnp.concatenate(packed, axis=1)
    packed_turned = [swing(whole)] if halving else turned(whole)
    part = (2 * side, width)
    if halving:
        first, second, third, fourth, own, parent = call(
            functools.partial(halving_kernel, columns, pcol // 2),
            (shape(part, BF), shape(part, BF), shape(part, F32), shape(part, F32))
            + (shape(part, F32), shape((side, side), BF)),
            [VMEM] * (3 * pcol // 2 + 2),
            [pltpu.VMEM((prow // 2, extent, 2 * side), BF)],
        )(*packed_all, near, other_known)
        first = trade(first, 0, 1, 1, 0)
        parent_other = trade(second, 0, 1, 1, 0)
        dense_turned = turn(packed_turned)
        first, dense_turned = lax.optimization_barrier((first, dense_turned))
        dense_turned = across(dense_turned, 2)
        third = trade(add(third, first), 2, 0, 1, 1)
        fourth = trade(add(fourth, parent_other), 2, 1, 1, 0)
        sums = [own, first, third, fourth]
    else:
        plan = rounds(prow, columns)
        outs = [shape((2 * side, width), F32)] + [shape((2 * side, width), BF)] * len(plan)
        *sums, parent = call(
            functools.partial(partial_kernel, plan, columns, pcol // 2),
            tuple(outs) + (shape((side, side), BF),),
            [VMEM] * (3 * pcol // 2 + 2),
            [
                pltpu.VMEM((prow // 2, extent, 2 * side), BF),
                pltpu.VMEM((2,) + known_inverse.shape, BF),
            ],
        )(*packed_all, near, other_known)
        sums = [sums[0]] + [send(x, *steps) for x, steps in zip(sums[1:], plan)]
        parent_other = across(parent, 1)
        dense_turned = turn(packed_turned)
    outs = [shape((side, width), BF)] * 2 + [shape((2, share, side), F32)]
    outs += [shape((2, share, side), BF)] * (pcol - 1)
    finished = call(
        functools.partial(finish_kernel, halving, len(sums), pcol, columns),
        tuple(outs),
        [VMEM] * (len(sums) + 4),
        [pltpu.VMEM((2, side, side), F32)],
    )(*sums, dense_turned, parent, parent_other, upper_pivots)
    upper_rows, lower_rows = finished[:2]
    pieces = [finished[2]] + [across(finished[2 + s], s) for s in range(1, pcol)]
    upper_diagonal, lower_diagonal = call(
        functools.partial(sum_kernel, pcol),
        (shape((share, side), F32), shape((share, side), F32)),
        [VMEM] * (pcol + 2),
    )(*pieces, upper_pivots, lower_pivots)
    return upper_rows, upper_diagonal, lower_rows, lower_diagonal


def solution(mesh):
    placed = (
        P(("pole", "prow"), "pcol"),
        P(("pole", "prow"), "pcol", None, None),
        P("prow", "pcol"),
        P(("pole", "prow", "pcol"), None),
        P(("pole", "prow"), "pcol", None, None),
        P("prow", "pcol"),
        P(("pole", "prow", "pcol"), None),
    )
    return jax.shard_map(
        per_device,
        mesh=mesh,
        in_specs=placed,
        out_specs=(
            P(("pole", "prow"), "pcol"),
            P(("pole", "prow", "pcol"), None),
            P(("pole", "prow"), "pcol"),
            P(("pole", "prow", "pcol"), None),
        ),
        check_vma=False,
    )
```

```python
import functools

import jax
import jax.numpy as jnp
from jax import lax
from jax.experimental import pallas as pl
from jax.experimental.pallas import tpu as pltpu
from jax.sharding import PartitionSpec as P

AR = 4
TURN_FLOPS = 1 << 28
NEAR_FLOPS = 1 << 30
BF = jnp.bfloat16
F32 = jnp.float32
VMEM = pl.BlockSpec(memory_space=pltpu.VMEM)
HBM = pl.BlockSpec(memory_space=pltpu.HBM)
SMEM = pl.BlockSpec(memory_space=pltpu.SMEM)


def tdot(a, b):
    return lax.dot_general(a, b, (((0,), (0,)), ((), ())), preferred_element_type=F32)


def ndot(a, b):
    return lax.dot_general(a, b, (((1,), (0,)), ((), ())), preferred_element_type=F32)


def split(x):
    hi = x.astype(BF)
    return hi, (x - hi.astype(F32)).astype(BF)


def lay(dense, panel, slots_ref, level):
    side = panel.shape[-1]
    slots = slots_ref[...].astype(F32)
    for v in range(AR):
        total = None
        for s in range(AR):
            index = level * AR + s
            chosen = (slots[index : index + 1] == v).astype(BF)
            term = panel[s * side : (s + 1) * side, :] * chosen
            total = term if total is None else total + term
        dense[v * side : (v + 1) * side, :] = total


def copy_kernel(known, near):
    near[...] = known[...]


def holder(k, columns):
    return (k // columns) % 2


def rounds(prow, columns):
    sends = [(t, e) for t in range(prow) for e in range(2) if (t, e) != (0, 0)]
    lists = {}
    for t, e in sends:
        lists.setdefault(((t // columns) % 2, e), []).append((t, e))
    out = []
    for e in range(2):
        even, odd = lists[0, e][::-1], lists[1, 1 - e][::-1]
        for n in range(max(len(even), len(odd))):
            out.append((even[n] if n < len(even) else None, odd[n] if n < len(odd) else None))
    return out


def partial_kernel(plan, columns, halves, *refs):
    panels = refs[:halves], refs[halves : 2 * halves]
    slots, refs = refs[2 * halves : 3 * halves], refs[3 * halves :]
    own_known, other_known, refs = refs[0], refs[1], refs[2:]
    own, refs = refs[0], refs[1:]
    outs, refs = refs[: len(plan)], refs[len(plan) :]
    parent, dense, known = refs
    r = lax.axis_index("prow")
    c = lax.axis_index("pcol")
    side = parent.shape[0]
    extent = AR * side
    holds = c % 2 == holder(r, columns)

    def slot(k):
        return k // (2 * columns) * columns + k % columns

    known[0] = own_known[...]
    known[1] = other_known[...]
    for j in range(halves):
        for i in range(columns):
            k = (c ^ (2 * j)) * columns + i
            for level in range(2):
                columns_of = pl.ds(level * side, side)
                lay(dense.at[slot(k), :, columns_of], panels[level][j].at[i], slots[j].at[i], level)

            @pl.when(k == r)
            def _():
                parent[...] = panels[1][j][i, :side]

    for n, (even, odd) in enumerate(plan):

        def put(t, e):
            outs[n][...] = tdot(dense[slot(r ^ t)], known[e]).astype(BF)

        if even is None or odd is None:

            @pl.when(holds if odd is None else jnp.logical_not(holds))
            def _():
                put(*(even or odd))

        else:
            put(jnp.where(holds, even[0], odd[0]), jnp.where(holds, even[1], odd[1]))

    @pl.when(holds)
    def _():
        own[...] = tdot(dense[slot(r)], own_known[...])

    @pl.when(jnp.logical_not(holds))
    def _():
        own[...] = jnp.zeros_like(own)
        parent[...] = jnp.zeros_like(parent)


def halving_kernel(columns, halves, *refs):
    panels = refs[:halves], refs[halves : 2 * halves]
    slots, refs = refs[2 * halves : 3 * halves], refs[3 * halves :]
    own_known, other_known, first, second, third, fourth, own, parent, dense = refs
    r = lax.axis_index("prow")
    c = lax.axis_index("pcol")
    side = parent.shape[0]
    extent = AR * side
    holds = c % 2 == holder(r, columns)

    def slot(k):
        return k // (2 * columns) * columns + k % columns

    for j in range(halves):
        for i in range(columns):
            k = (c ^ (2 * j)) * columns + i
            for level in range(2):
                columns_of = pl.ds(level * side, side)
                lay(dense.at[slot(k), :, columns_of], panels[level][j].at[i], slots[j].at[i], level)

            @pl.when(k == r)
            def _():
                parent[...] = panels[1][j][i, :side]

    @pl.when(holds)
    def _():
        panel = dense[slot(r)]
        first[...] = tdot(panel, other_known[...]).astype(BF)
        own[...] = tdot(panel, own_known[...])
        second[:side, :side] = parent[...]
        panel = dense[slot(r ^ 2)]
        third[...] = tdot(panel, own_known[...])
        fourth[...] = tdot(panel, other_known[...])

    @pl.when(jnp.logical_not(holds))
    def _():
        panel = dense[slot(r ^ 3)]
        first[...] = tdot(panel, own_known[...]).astype(BF)
        second[...] = tdot(panel, other_known[...]).astype(BF)
        panel = dense[slot(r ^ 1)]
        third[...] = tdot(panel, other_known[...])
        fourth[...] = tdot(panel, own_known[...])


def add_kernel(columns, kept, arrived, total):
    holds = lax.axis_index("pcol") % 2 == holder(lax.axis_index("prow"), columns)

    @pl.when(holds)
    def _():
        total[...] = (kept[...] + arrived[...].astype(F32)).astype(BF)

    @pl.when(jnp.logical_not(holds))
    def _():
        total[...] = kept[...].astype(BF)


def turn_kernel(level, columns, *refs):
    turned, dense = refs[:-1], refs[-1]
    r = lax.axis_index("prow")
    side = dense.shape[1]
    extent = AR * side
    for p in range(columns):
        q = (r - p) % columns if columns > 1 else 0
        rows = pl.ds(pl.multiple_of(q * extent, extent), extent)
        panel = turned[p].at[0, pl.ds(0, extent), :]
        slots = turned[p].at[0, pl.ds(extent, 4 * AR), :]
        lay(dense.at[rows, :], panel, slots, level)


def finish_kernel(halving, count, pcol, columns, *refs):
    sums, refs = refs[:count], refs[count:]
    dense, refs = (refs[0], refs[1]), refs[2:]
    parent_ref, parent_other, pivots, refs = refs[0], refs[1], refs[2], refs[3:]
    upper_rows, lower_rows, refs = refs[0], refs[1], refs[2:]
    pieces, refs = refs[:pcol], refs[pcol:]
    parts = refs[0]
    r = lax.axis_index("prow")
    c = lax.axis_index("pcol")
    side = parent_ref.shape[0]
    share = pivots.shape[0]
    if halving:
        holds = c % 2 == holder(r, columns)
        parent = jnp.where(holds, parent_ref[...], parent_other[:side, :side])
        total = jnp.where(holds, sums[0][...], sums[1][...].astype(F32))
        total += sums[2][...].astype(F32) + sums[3][...].astype(F32)
    else:
        parent = parent_ref[...] + parent_other[...]
        total = sums[0][...]
        for t in range(1, count):
            total += sums[t][...].astype(F32)
    upper_sum, lower_sum = total[:side], total[side:]
    hi, lo = split(upper_sum)
    rows = -hi
    upper_rows[...] = rows
    upper_part = ndot(hi, dense[0][...]) + ndot(lo, dense[0][...])
    parts[0] = upper_part
    parts[1] = upper_part
    own = pl.ds(pl.multiple_of(c * share, share), share)
    parts[1, own, :] += pivots[...]
    lower_sum += tdot(parent, rows)
    hi, lo = split(lower_sum)
    lower_rows[...] = -hi
    lower_part = ndot(hi, dense[1][...]) + ndot(lo, dense[1][...])
    coupling_hi, coupling_lo = split(ndot(rows, dense[1][...]))
    lower_part += tdot(coupling_hi, parent) + tdot(coupling_lo, parent)
    hi, lo = split(parts[1])
    hi, lo = split(ndot(hi, parent) + ndot(lo, parent))
    parts[1] = lower_part + tdot(parent, hi) + tdot(parent, lo)
    for s in range(pcol):
        theirs = pl.ds(pl.multiple_of((c ^ s) * share, share), share)
        pieces[s][0] = parts[0, theirs, :].astype(pieces[s].dtype)
        pieces[s][1] = parts[1, theirs, :].astype(pieces[s].dtype)


def sum_kernel(pcol, *refs):
    pieces, refs = refs[:pcol], refs[pcol:]
    upper_pivots, lower_pivots, upper_diagonal, lower_diagonal = refs
    total = pieces[0][...]
    for s in range(1, pcol):
        total += pieces[s][...].astype(F32)
    upper_diagonal[...] = upper_pivots[...] + total[0]
    lower_diagonal[...] = lower_pivots[...] + total[1]


def call(kernel, outs, specs, scratch=(), room=32, flops=0):
    return pl.pallas_call(
        kernel,
        out_shape=outs,
        in_specs=specs,
        out_specs=tuple(VMEM for _ in outs),
        scratch_shapes=scratch,
        cost_estimate=pl.CostEstimate(flops=flops, bytes_accessed=0, transcendentals=0),
        compiler_params=pltpu.CompilerParams(vmem_limit_bytes=room << 20),
    )


def per_device(
    known_inverse, upper_panel, upper_slots, upper_pivots, lower_panel, lower_slots, lower_pivots
):
    prow = lax.axis_size("prow")
    pcol = lax.axis_size("pcol")
    columns = upper_panel.shape[1]
    side = upper_panel.shape[2]
    width = known_inverse.shape[1]
    extent = AR * side
    share = upper_pivots.shape[0]
    shape = jax.ShapeDtypeStruct

    def across(x, j):
        return lax.ppermute(x, "pcol", [(c, c ^ j) for c in range(pcol)])

    def flat(r, c):
        return r * pcol + c

    def send(x, even, odd):
        pairs = []
        for r in range(prow):
            for c in range(pcol):
                step = even if c % 2 == holder(r, columns) else odd
                if step is not None:
                    pairs.append((flat(r, c), flat(r ^ step[0], c ^ step[1])))
        return lax.ppermute(x, ("prow", "pcol"), pairs)

    def swing(x):
        pairs = []
        for a in range(prow):
            for b in range(pcol):
                c = a ^ 2 if a // 2 == b // 2 else b // 2 * 2 + a % 2
                pairs.append((flat(a, b), flat(b, c)))
        return lax.ppermute(x, ("prow", "pcol"), pairs)

    def trade(x, held_step, held_other, step, other):
        pairs = []
        for r in range(prow):
            for c in range(pcol):
                if c % 2 == holder(r, columns):
                    pairs.append((flat(r, c), flat(r ^ held_step, c ^ held_other)))
                else:
                    pairs.append((flat(r, c), flat(r ^ step, c ^ other)))
        return lax.ppermute(x, ("prow", "pcol"), pairs)

    def add(kept, arrived):
        out = (shape(arrived.shape, BF),)
        return call(functools.partial(add_kernel, columns), out, [VMEM] * 2)(kept, arrived)[0]

    def turn(moved, level):
        return call(
            functools.partial(turn_kernel, level, columns),
            (shape((width, side), BF),),
            [VMEM] * columns,
            flops=(2 << 30) if level == 0 else (3 << 30),
        )(*moved)[0]

    def turned(x):
        moved = []
        for p in range(columns):
            pairs = []
            for a in range(prow):
                for b in range(pcol):
                    pairs.append((a * pcol + b, (b * columns + (a + p) % columns) * pcol + a // columns))
            piece = x
            if columns > 1:
                first = (lax.axis_index("prow") + p) % columns
                piece = lax.dynamic_slice_in_dim(x, first, 1, 0)
            moved.append(lax.ppermute(piece, ("prow", "pcol"), pairs))
        return moved

    slots = jnp.concatenate([upper_slots, lower_slots, lower_slots, lower_slots], axis=0).T
    packed = [
        jnp.swapaxes(upper_panel, 0, 1).reshape(columns, extent, side),
        jnp.swapaxes(lower_panel, 0, 1).reshape(columns, extent, side),
        jnp.broadcast_to(slots[:, :, None].astype(BF), (columns, 4 * AR, side)),
    ]
    packed_all = []
    for x in packed:
        packed_all += [x] + [across(x, j) for j in range(2, pcol, 2)]
    other_known = across(known_inverse, 1)
    near = call(copy_kernel, (shape(known_inverse.shape, BF),), [VMEM], flops=NEAR_FLOPS)(known_inverse)[0]
    halving = prow == 4 and columns == 1
    upper_turned = jnp.concatenate([packed[0], packed[2]], axis=1)
    upper_turned = [swing(upper_turned)] if halving else turned(upper_turned)
    lower_turned = turned(jnp.concatenate([packed[1], packed[2]], axis=1))
    part = (2 * side, width)
    if halving:
        first, second, third, fourth, own, parent = call(
            functools.partial(halving_kernel, columns, pcol // 2),
            (shape(part, BF), shape(part, BF), shape(part, F32), shape(part, F32))
            + (shape(part, F32), shape((side, side), BF)),
            [VMEM] * (3 * pcol // 2 + 2),
            [pltpu.VMEM((prow // 2, extent, 2 * side), BF)],
        )(*packed_all, near, other_known)
        first = trade(first, 0, 1, 1, 0)
        parent_other = trade(second, 0, 1, 1, 0)
        swung = turn(upper_turned, 0)
        first, swung = lax.optimization_barrier((first, swung))
        upper_dense = across(swung, 2)
        third = trade(add(third, first), 2, 0, 1, 1)
        fourth = trade(add(fourth, parent_other), 2, 1, 1, 0)
        lower_dense = turn(lower_turned, 1)
        sums = [own, first, third, fourth]
    else:
        plan = rounds(prow, columns)
        outs = [shape((2 * side, width), F32)] + [shape((2 * side, width), BF)] * len(plan)
        *sums, parent = call(
            functools.partial(partial_kernel, plan, columns, pcol // 2),
            tuple(outs) + (shape((side, side), BF),),
            [VMEM] * (3 * pcol // 2 + 2),
            [
                pltpu.VMEM((prow // 2, extent, 2 * side), BF),
                pltpu.VMEM((2,) + known_inverse.shape, BF),
            ],
        )(*packed_all, near, other_known)
        sums = [sums[0]] + [send(x, *steps) for x, steps in zip(sums[1:], plan)]
        parent_other = across(parent, 1)
        upper_dense, lower_dense = turn(upper_turned, 0), turn(lower_turned, 1)
    outs = [shape((side, width), BF)] * 2 + [shape((2, share, side), F32)]
    outs += [shape((2, share, side), BF)] * (pcol - 1)
    finished = call(
        functools.partial(finish_kernel, halving, len(sums), pcol, columns),
        tuple(outs),
        [VMEM] * (len(sums) + 5),
        [pltpu.VMEM((2, side, side), F32)],
    )(*sums, upper_dense, lower_dense, parent, parent_other, upper_pivots)
    upper_rows, lower_rows = finished[:2]
    pieces = [finished[2]] + [across(finished[2 + s], s) for s in range(1, pcol)]
    upper_diagonal, lower_diagonal = call(
        functools.partial(sum_kernel, pcol),
        (shape((share, side), F32), shape((share, side), F32)),
        [VMEM] * (pcol + 2),
    )(*pieces, upper_pivots, lower_pivots)
    return upper_rows, upper_diagonal, lower_rows, lower_diagonal


def solution(mesh):
    placed = (
        P(("pole", "prow"), "pcol"),
        P(("pole", "prow"), "pcol", None, None),
        P("prow", "pcol"),
        P(("pole", "prow", "pcol"), None),
        P(("pole", "prow"), "pcol", None, None),
        P("prow", "pcol"),
        P(("pole", "prow", "pcol"), None),
    )
    return jax.shard_map(
        per_device,
        mesh=mesh,
        in_specs=placed,
        out_specs=(
            P(("pole", "prow"), "pcol"),
            P(("pole", "prow", "pcol"), None),
            P(("pole", "prow"), "pcol"),
            P(("pole", "prow", "pcol"), None),
        ),
        check_vma=False,
    )
```

```python
import functools

import jax
import jax.numpy as jnp
from jax import lax
from jax.experimental import pallas as pl
from jax.experimental.pallas import tpu as pltpu
from jax.sharding import PartitionSpec as P

AR = 4
TURN_FLOPS = 1 << 28
NEAR_FLOPS = 1 << 30
BF = jnp.bfloat16
F32 = jnp.float32
VMEM = pl.BlockSpec(memory_space=pltpu.VMEM)
HBM = pl.BlockSpec(memory_space=pltpu.HBM)
SMEM = pl.BlockSpec(memory_space=pltpu.SMEM)


def tdot(a, b):
    return lax.dot_general(a, b, (((0,), (0,)), ((), ())), preferred_element_type=F32)


def ndot(a, b):
    return lax.dot_general(a, b, (((1,), (0,)), ((), ())), preferred_element_type=F32)


def split(x):
    hi = x.astype(BF)
    return hi, (x - hi.astype(F32)).astype(BF)


def lay(dense, panel, slots_ref, level):
    side = panel.shape[-1]
    slots = slots_ref[...].astype(F32)
    for v in range(AR):
        total = None
        for s in range(AR):
            index = level * AR + s
            chosen = (slots[index : index + 1] == v).astype(BF)
            term = panel[s * side : (s + 1) * side, :] * chosen
            total = term if total is None else total + term
        dense[v * side : (v + 1) * side, :] = total


def copy_kernel(known, near):
    near[...] = known[...]


def holder(k, columns):
    return (k // columns) % 2


def rounds(prow, columns):
    sends = [(t, e) for t in range(prow) for e in range(2) if (t, e) != (0, 0)]
    lists = {}
    for t, e in sends:
        lists.setdefault(((t // columns) % 2, e), []).append((t, e))
    out = []
    for e in range(2):
        even, odd = lists[0, e][::-1], lists[1, 1 - e][::-1]
        for n in range(max(len(even), len(odd))):
            out.append((even[n] if n < len(even) else None, odd[n] if n < len(odd) else None))
    return out


def partial_kernel(plan, columns, halves, *refs):
    panels = refs[:halves], refs[halves : 2 * halves]
    slots, refs = refs[2 * halves : 3 * halves], refs[3 * halves :]
    own_known, other_known, refs = refs[0], refs[1], refs[2:]
    own, refs = refs[0], refs[1:]
    outs, refs = refs[: len(plan)], refs[len(plan) :]
    parent, dense, known = refs
    r = lax.axis_index("prow")
    c = lax.axis_index("pcol")
    side = parent.shape[0]
    extent = AR * side
    holds = c % 2 == holder(r, columns)

    def slot(k):
        return k // (2 * columns) * columns + k % columns

    known[0] = own_known[...]
    known[1] = other_known[...]
    for j in range(halves):
        for i in range(columns):
            k = (c ^ (2 * j)) * columns + i
            for level in range(2):
                columns_of = pl.ds(level * side, side)
                lay(dense.at[slot(k), :, columns_of], panels[level][j].at[i], slots[j].at[i], level)

            @pl.when(k == r)
            def _():
                parent[...] = panels[1][j][i, :side]

    for n, (even, odd) in enumerate(plan):

        def put(t, e):
            outs[n][...] = tdot(dense[slot(r ^ t)], known[e]).astype(BF)

        if even is None or odd is None:

            @pl.when(holds if odd is None else jnp.logical_not(holds))
            def _():
                put(*(even or odd))

        else:
            put(jnp.where(holds, even[0], odd[0]), jnp.where(holds, even[1], odd[1]))

    @pl.when(holds)
    def _():
        own[...] = tdot(dense[slot(r)], own_known[...])

    @pl.when(jnp.logical_not(holds))
    def _():
        own[...] = jnp.zeros_like(own)
        parent[...] = jnp.zeros_like(parent)


def take(columns, halves, refs, k, dense, parent=None):
    panels = refs[:halves], refs[halves : 2 * halves]
    slots = refs[2 * halves : 3 * halves]
    side = dense.shape[1] // 2
    for j in range(halves):
        for i in range(columns):

            @pl.when((lax.axis_index("pcol") ^ (2 * j)) * columns + i == k)
            def _():
                for level in range(2):
                    columns_of = pl.ds(level * side, side)
                    lay(dense.at[:, columns_of], panels[level][j].at[i], slots[j].at[i], level)
                if parent is not None:
                    parent[...] = panels[1][j][i, :side]


def leading_kernel(columns, halves, *refs):
    own_known, other_known, first, second, parent, dense = refs[3 * halves :]
    r = lax.axis_index("prow")
    side = parent.shape[0]
    holds = lax.axis_index("pcol") % 2 == holder(r, columns)
    take(columns, halves, refs, r ^ jnp.where(holds, 0, 3), dense, parent)

    @pl.when(holds)
    def _():
        first[...] = tdot(dense[...], other_known[...]).astype(BF)
        second[:side, :side] = parent[...]

    @pl.when(jnp.logical_not(holds))
    def _():
        first[...] = tdot(dense[...], other_known[...]).astype(BF)
        second[...] = tdot(dense[...], own_known[...]).astype(BF)


def trailing_kernel(columns, halves, *refs):
    own_known, other_known, third, fourth, own, dense = refs[3 * halves :]
    r = lax.axis_index("prow")
    holds = lax.axis_index("pcol") % 2 == holder(r, columns)
    take(columns, halves, refs, r ^ jnp.where(holds, 2, 1), dense)

    @pl.when(holds)
    def _():
        third[...] = tdot(dense[...], other_known[...])
        fourth[...] = tdot(dense[...], own_known[...])
        take(columns, halves, refs, r, dense)
        own[...] = tdot(dense[...], own_known[...])

    @pl.when(jnp.logical_not(holds))
    def _():
        third[...] = tdot(dense[...], own_known[...])
        fourth[...] = tdot(dense[...], other_known[...])


def add_kernel(columns, kept, arrived, total):
    holds = lax.axis_index("pcol") % 2 == holder(lax.axis_index("prow"), columns)

    @pl.when(holds)
    def _():
        total[...] = (kept[...] + arrived[...].astype(F32)).astype(BF)

    @pl.when(jnp.logical_not(holds))
    def _():
        total[...] = kept[...].astype(BF)


def turn_kernel(level, columns, *refs):
    turned, dense = refs[:-1], refs[-1]
    r = lax.axis_index("prow")
    side = dense.shape[1]
    extent = AR * side
    for p in range(columns):
        q = (r - p) % columns if columns > 1 else 0
        rows = pl.ds(pl.multiple_of(q * extent, extent), extent)
        panel = turned[p].at[0, pl.ds(0, extent), :]
        slots = turned[p].at[0, pl.ds(extent, 4 * AR), :]
        lay(dense.at[rows, :], panel, slots, level)


def whole_sums(halving, columns, sums, parent_ref, parent_other):
    side = parent_ref.shape[0]
    holds = lax.axis_index("pcol") % 2 == holder(lax.axis_index("prow"), columns)
    if halving:
        parent = jnp.where(holds, parent_ref[...], parent_other[:side, :side])
        total = jnp.where(holds, sums[0][...], sums[1][...].astype(F32))
        total += sums[2][...].astype(F32) + sums[3][...].astype(F32)
    else:
        parent = parent_ref[...] + parent_other[...]
        total = sums[0][...]
        for t in range(1, len(sums)):
            total += sums[t][...].astype(F32)
    rows = -total[:side].astype(BF)
    return parent, rows, total[:side], total[side:] + tdot(parent, rows)


def rows_kernel(halving, count, columns, *refs):
    sums, (parent_ref, parent_other, upper_rows, lower_rows) = refs[:count], refs[count:]
    _, rows, _, lower_sum = whole_sums(halving, columns, sums, parent_ref, parent_other)
    upper_rows[...] = rows
    lower_rows[...] = -lower_sum.astype(BF)


def finish_kernel(halving, count, pcol, columns, *refs):
    sums, refs = refs[:count], refs[count:]
    dense, refs = (refs[0], refs[1]), refs[2:]
    parent_ref, parent_other, pivots, refs = refs[0], refs[1], refs[2], refs[3:]
    pieces, refs = refs[:pcol], refs[pcol:]
    parts = refs[0]
    c = lax.axis_index("pcol")
    share = pivots.shape[0]
    parent, rows, upper_sum, lower_sum = whole_sums(
        halving, columns, sums, parent_ref, parent_other
    )
    hi, lo = split(upper_sum)
    upper_part = ndot(hi, dense[0][...]) + ndot(lo, dense[0][...])
    parts[0] = upper_part
    parts[1] = upper_part
    own = pl.ds(pl.multiple_of(c * share, share), share)
    parts[1, own, :] += pivots[...]
    hi, lo = split(lower_sum)
    lower_part = ndot(hi, dense[1][...]) + ndot(lo, dense[1][...])
    coupling_hi, coupling_lo = split(ndot(rows, dense[1][...]))
    lower_part += tdot(coupling_hi, parent) + tdot(coupling_lo, parent)
    hi, lo = split(parts[1])
    hi, lo = split(ndot(hi, parent) + ndot(lo, parent))
    parts[1] = lower_part + tdot(parent, hi) + tdot(parent, lo)
    for s in range(pcol):
        theirs = pl.ds(pl.multiple_of((c ^ s) * share, share), share)
        pieces[s][0] = parts[0, theirs, :].astype(pieces[s].dtype)
        pieces[s][1] = parts[1, theirs, :].astype(pieces[s].dtype)


def sum_kernel(pcol, *refs):
    pieces, refs = refs[:pcol], refs[pcol:]
    upper_pivots, lower_pivots, upper_diagonal, lower_diagonal = refs
    total = pieces[0][...]
    for s in range(1, pcol):
        total += pieces[s][...].astype(F32)
    upper_diagonal[...] = upper_pivots[...] + total[0]
    lower_diagonal[...] = lower_pivots[...] + total[1]


def call(kernel, outs, specs, scratch=(), room=32, flops=0):
    return pl.pallas_call(
        kernel,
        out_shape=outs,
        in_specs=specs,
        out_specs=tuple(VMEM for _ in outs),
        scratch_shapes=scratch,
        cost_estimate=pl.CostEstimate(flops=flops, bytes_accessed=0, transcendentals=0),
        compiler_params=pltpu.CompilerParams(vmem_limit_bytes=room << 20),
    )


def per_device(
    known_inverse, upper_panel, upper_slots, upper_pivots, lower_panel, lower_slots, lower_pivots
):
    prow = lax.axis_size("prow")
    pcol = lax.axis_size("pcol")
    columns = upper_panel.shape[1]
    side = upper_panel.shape[2]
    width = known_inverse.shape[1]
    extent = AR * side
    share = upper_pivots.shape[0]
    shape = jax.ShapeDtypeStruct

    def across(x, j):
        return lax.ppermute(x, "pcol", [(c, c ^ j) for c in range(pcol)])

    def flat(r, c):
        return r * pcol + c

    def send(x, even, odd):
        pairs = []
        for r in range(prow):
            for c in range(pcol):
                step = even if c % 2 == holder(r, columns) else odd
                if step is not None:
                    pairs.append((flat(r, c), flat(r ^ step[0], c ^ step[1])))
        return lax.ppermute(x, ("prow", "pcol"), pairs)

    def swing(x):
        pairs = []
        for a in range(prow):
            for b in range(pcol):
                c = a ^ 2 if a // 2 == b // 2 else b // 2 * 2 + a % 2
                pairs.append((flat(a, b), flat(b, c)))
        return lax.ppermute(x, ("prow", "pcol"), pairs)

    def trade(x, held_step, held_other, step, other):
        pairs = []
        for r in range(prow):
            for c in range(pcol):
                if c % 2 == holder(r, columns):
                    pairs.append((flat(r, c), flat(r ^ held_step, c ^ held_other)))
                else:
                    pairs.append((flat(r, c), flat(r ^ step, c ^ other)))
        return lax.ppermute(x, ("prow", "pcol"), pairs)

    def add(kept, arrived):
        out = (shape(arrived.shape, BF),)
        return call(functools.partial(add_kernel, columns), out, [VMEM] * 2)(kept, arrived)[0]

    def turn(moved, level):
        return call(
            functools.partial(turn_kernel, level, columns),
            (shape((width, side), BF),),
            [VMEM] * columns,
            flops=(2 << 30) if level == 0 else (3 << 30),
        )(*moved)[0]

    def turned(x):
        moved = []
        for p in range(columns):
            pairs = []
            for a in range(prow):
                for b in range(pcol):
                    pairs.append((a * pcol + b, (b * columns + (a + p) % columns) * pcol + a // columns))
            piece = x
            if columns > 1:
                first = (lax.axis_index("prow") + p) % columns
                piece = lax.dynamic_slice_in_dim(x, first, 1, 0)
            moved.append(lax.ppermute(piece, ("prow", "pcol"), pairs))
        return moved

    slots = jnp.concatenate([upper_slots, lower_slots, lower_slots, lower_slots], axis=0).T
    packed = [
        jnp.swapaxes(upper_panel, 0, 1).reshape(columns, extent, side),
        jnp.swapaxes(lower_panel, 0, 1).reshape(columns, extent, side),
        jnp.broadcast_to(slots[:, :, None].astype(BF), (columns, 4 * AR, side)),
    ]
    packed_all = []
    for x in packed:
        packed_all += [x] + [across(x, j) for j in range(2, pcol, 2)]
    other_known = across(known_inverse, 1)
    near = call(copy_kernel, (shape(known_inverse.shape, BF),), [VMEM], flops=NEAR_FLOPS)(known_inverse)[0]
    halving = prow == 4 and columns == 1
    upper_turned = jnp.concatenate([packed[0], packed[2]], axis=1)
    upper_turned = [swing(upper_turned)] if halving else turned(upper_turned)
    lower_turned = turned(jnp.concatenate([packed[1], packed[2]], axis=1))
    part = (2 * side, width)
    if halving:
        operands = (*packed_all, near, other_known)
        first, second, parent = call(
            functools.partial(leading_kernel, columns, pcol // 2),
            (shape(part, BF), shape(part, BF), shape((side, side), BF)),
            [VMEM] * (3 * pcol // 2 + 2),
            [pltpu.VMEM((extent, 2 * side), BF)],
        )(*operands)
        third, fourth, own = call(
            functools.partial(trailing_kernel, columns, pcol // 2),
            (shape(part, F32), shape(part, F32), shape(part, F32)),
            [VMEM] * (3 * pcol // 2 + 2),
            [pltpu.VMEM((extent, 2 * side), BF)],
        )(*operands)
        first = trade(first, 0, 1, 1, 0)
        parent_other = trade(second, 0, 1, 1, 0)
        swung = turn(upper_turned, 0)
        first, swung = lax.optimization_barrier((first, swung))
        upper_dense = across(swung, 2)
        third = trade(add(third, first), 2, 1, 1, 0)
        fourth = trade(add(fourth, parent_other), 2, 0, 1, 1)
        lower_dense = turn(lower_turned, 1)
        sums = [own, first, third, fourth]
    else:
        plan = rounds(prow, columns)
        outs = [shape((2 * side, width), F32)] + [shape((2 * side, width), BF)] * len(plan)
        *sums, parent = call(
            functools.partial(partial_kernel, plan, columns, pcol // 2),
            tuple(outs) + (shape((side, side), BF),),
            [VMEM] * (3 * pcol // 2 + 2),
            [
                pltpu.VMEM((prow // 2, extent, 2 * side), BF),
                pltpu.VMEM((2,) + known_inverse.shape, BF),
            ],
        )(*packed_all, near, other_known)
        sums = [sums[0]] + [send(x, *steps) for x, steps in zip(sums[1:], plan)]
        parent_other = across(parent, 1)
        upper_dense, lower_dense = turn(upper_turned, 0), turn(lower_turned, 1)
    outs = [shape((2, share, side), F32)]
    outs += [shape((2, share, side), BF)] * (pcol - 1)
    finished = call(
        functools.partial(finish_kernel, halving, len(sums), pcol, columns),
        tuple(outs),
        [VMEM] * (len(sums) + 5),
        [pltpu.VMEM((2, side, side), F32)],
    )(*sums, upper_dense, lower_dense, parent, parent_other, upper_pivots)
    upper_rows, lower_rows = call(
        functools.partial(rows_kernel, halving, len(sums), columns),
        (shape((side, width), BF), shape((side, width), BF)),
        [VMEM] * (len(sums) + 2),
    )(*sums, parent, parent_other)
    pieces = [finished[0]] + [across(finished[s], s) for s in range(1, pcol)]
    upper_diagonal, lower_diagonal = call(
        functools.partial(sum_kernel, pcol),
        (shape((share, side), F32), shape((share, side), F32)),
        [VMEM] * (pcol + 2),
    )(*pieces, upper_pivots, lower_pivots)
    return upper_rows, upper_diagonal, lower_rows, lower_diagonal


def solution(mesh):
    placed = (
        P(("pole", "prow"), "pcol"),
        P(("pole", "prow"), "pcol", None, None),
        P("prow", "pcol"),
        P(("pole", "prow", "pcol"), None),
        P(("pole", "prow"), "pcol", None, None),
        P("prow", "pcol"),
        P(("pole", "prow", "pcol"), None),
    )
    return jax.shard_map(
        per_device,
        mesh=mesh,
        in_specs=placed,
        out_specs=(
            P(("pole", "prow"), "pcol"),
            P(("pole", "prow", "pcol"), None),
            P(("pole", "prow"), "pcol"),
            P(("pole", "prow", "pcol"), None),
        ),
        check_vma=False,
    )
```
